32 devices in a mesh: groups: 2 (over y), fsdp: 4 (over z), mp: 2 (over x), sub: 2 (over core).
Axes of the slice: x: 2, y: 2, z: 4, core: 2. Of those that a mesh axis runs over, the one named last changes fastest.
Arguments:
- queries: bfloat16 [4096, 16384], P(('groups', 'fsdp', 'sub'), 'mp'), parts along dimension 0, may hold values from -68 to 68
- lengths: int32 [8], P('groups'), parts along dimension 0, may hold values from 1 to 512, 1024 in all
- prompt_x: bfloat16 [4096, 16384], P(('groups', 'fsdp', 'sub'), 'mp'), parts along dimension 0, may hold values from -6 to 6
- norm_gain: float32 [16384], replicated, may hold values from 0.1 to 1.9
- key_weight: bfloat16 [16384, 1024], P(('fsdp', 'sub'), 'mp'), may hold values from -0.046875 to 0.046875
- value_weight: bfloat16 [16384, 1024], P(('fsdp', 'sub'), 'mp'), may hold values from -0.046875 to 0.046875
Outputs:
- prefix_out: bfloat16 [4096, 16384], P(('groups', 'fsdp', 'sub'), 'mp'), parts along dimension 0
- prefix_lse: float32 [4096, 128], P(('groups', 'fsdp', 'sub'), 'mp'), parts along dimension 0
The draws below stay inside these ranges and needn't reach their ends.
There are 2 independent parts, one for each index of `groups`. The reference program is written for one: setup_inputs(seed, part) draws one part's arguments, and reference() takes and returns one part's arrays. A program takes and returns all parts, laid end to end along the dimension named above; an argument that names none is the same for every part. Nothing has to cross between parts.
Inputs may be any that keep to these rules, and one draw needn't show every extreme that they name: The 4 lengths of a part sum to exactly 1024, and the largest is 512.
All inputs are finite; a program needn't handle non-finite values.
Results may differ from the reference program's by a relative error of at most 0.009.
The reference program's roundings to bfloat16 on the way (of `normed`, `cache_values`, `cache_keys` and `weights`) count: a program that leaves them out, or rounds other values in their place, can miss the bound.
Values may be sent and summed in bfloat16 or wider, within the bound.
A program may use at most 128 MiB of HBM per device.

```python
import math
import jax
import jax.numpy as jnp
import numpy as np
from jax import lax

D = 16384
HQ = 128
KVH = 8
HD = 128
COMPL = 4
PROMPT = 2048
LMAX = 512
ROWS = 2048


def draw_queries(key, part):
    key = jax.random.fold_in(key, 11)
    base_key, scale_key = jax.random.split(key)
    base = jnp.clip(jax.random.normal(base_key, (ROWS, HQ, HD), jnp.float32), -4.0, 4.0)
    scales = jnp.exp(jax.random.uniform(scale_key, (ROWS, HQ, 1), jnp.float32, math.log(0.5), math.log(3.0)))
    return (base * scales).reshape(ROWS, HQ * HD).astype(jnp.bfloat16)


def levels(rng, shape, cuts, least, high):
    gain = 1.0
    for position, blocks in cuts:
        steps = jax.random.uniform(jax.random.fold_in(jax.random.fold_in(rng, 6), position), (blocks,), jnp.float32, least / len(cuts), high / len(cuts))
        gain = gain * jnp.repeat(jnp.exp(steps), shape[position] // blocks).reshape((-1,) + (1,) * (len(shape) - 1 - position))
    return gain


def profile(count, total, bound, skew):
    portions = [(1 << 20) // math.isqrt(rank ** skew) + 1 for rank in range(2, count + 1)]
    spare, counts = total - bound - (count - 1), [1] * (count - 1)
    while spare > 0:
        free = [i for i in range(count - 1) if counts[i] < bound]
        pool, remaining = sum([portions[i] for i in free]), spare
        for i in free:
            more = min(bound - counts[i], max(1, remaining * portions[i] // pool), spare)
            counts[i] = counts[i] + more
            spare = spare - more
    return np.array([bound] + counts)


def uneven(stream_key, count, total, limit, slope):
    if count == 2:
        one = jax.random.randint(stream_key, (), max(1, total - limit), min(limit, total - 1) + 1)
        return jnp.stack([one, total - one])
    sizes = jnp.asarray(profile(count, total, limit, slope), jnp.int32)
    twos = (count - 1) // 2
    donor, receiver = sizes[1:1 + 2 * twos:2], sizes[2:2 + 2 * twos:2]
    room = jnp.minimum(donor - 1, limit - receiver)
    moved = jax.random.randint(jax.random.fold_in(stream_key, 1), (twos,), 0, 1 << 20) % (room + 1)
    sizes = sizes.at[1:1 + 2 * twos:2].set(donor - moved).at[2:2 + 2 * twos:2].set(receiver + moved)
    return sizes[jax.random.permutation(jax.random.fold_in(stream_key, 2), count)]


def centred(own_key, extent, spread, bound, shards=(), kind=jnp.bfloat16):
    array = jax.random.normal(own_key, extent, jnp.float32) * spread
    if len(shards) > 0:
        array = levels(own_key, extent, shards, -0.22, 0.18) * array
    return jnp.clip(array, min=-bound, max=bound).astype(kind)


def setup_inputs(seed: int = 0, part: int = 0) -> dict:
    key_of = jax.random.split(jax.random.key(seed), 7)
    own_keys = jax.random.split(jax.random.fold_in(key_of[6], part), 7)
    queries = draw_queries(jax.random.fold_in(jax.random.fold_in(key_of[6], part), 71), part)
    lengths = uneven(own_keys[1], COMPL, 2 * LMAX, LMAX, 2).astype(jnp.int32)
    prompt_x = centred(own_keys[2], (PROMPT, D), 1.0, 6.0, ((0, 8), (1, 2)))
    norm_gain = jnp.clip(1.0 + 0.18 * jax.random.normal(key_of[3], (D,), jnp.float32), 0.1, 1.9)
    key_weight = centred(key_of[4], (D, KVH * HD), D ** -0.5, 0.046875, ((0, 8), (1, 2)))
    value_weight = centred(key_of[5], (D, KVH * HD), D ** -0.5, 0.046875, ((0, 8), (1, 2)))
    return dict(queries=queries, lengths=lengths, prompt_x=prompt_x, norm_gain=norm_gain, key_weight=key_weight, value_weight=value_weight)


rope_base = 500000.0
norm_eps = 1e-05

def rotate(field, positions):
    half = field.shape[-1] // 2
    exponents = jnp.arange(half, dtype=jnp.float32) * (2.0 / field.shape[-1])
    freqs = jnp.exp(-exponents * jnp.log(jnp.float32(rope_base)))
    angles = positions.astype(jnp.float32)[:, None] * freqs[None, :]
    cosine = jnp.cos(angles)[:, None, :]
    sine = jnp.sin(angles)[:, None, :]
    first = field[..., :half]
    second = field[..., half:]
    return jnp.concatenate([first * cosine - second * sine, second * cosine + first * sine], axis=-1)

def reference(queries, lengths, prompt_x, norm_gain, key_weight, value_weight):
    widened = prompt_x.astype(jnp.float32)
    mean_square = lax.optimization_barrier(jnp.mean(widened * widened, axis=1, keepdims=True))
    normed = (widened * lax.rsqrt(mean_square + norm_eps) * norm_gain[None, :]).astype(jnp.bfloat16)
    raw_keys = jnp.dot(normed, key_weight, preferred_element_type=jnp.float32)
    raw_values = jnp.dot(normed, value_weight, preferred_element_type=jnp.float32)
    positions = jnp.arange(PROMPT, dtype=jnp.int32)
    rounded_keys = rotate(raw_keys.reshape(PROMPT, KVH, HD), positions).astype(jnp.bfloat16)
    rounded_values = raw_values.reshape(PROMPT, KVH, HD).astype(jnp.bfloat16)
    cache_keys = lax.optimization_barrier(rounded_keys).astype(jnp.float32)
    cache_values = lax.optimization_barrier(rounded_values).astype(jnp.float32)
    group = HQ // KVH
    block = 64 if ROWS % 64 == 0 else ROWS
    blocks = queries.reshape(ROWS // block, block, KVH, group, HD)

    def attend_block(query_block):
        widened_q = query_block.astype(jnp.float32)
        scores = jnp.einsum('rkgd,pkd->rkgp', widened_q, cache_keys) * HD ** (-0.5)
        peak = lax.optimization_barrier(jnp.max(scores, axis=-1, keepdims=True))
        expd = jnp.exp(scores - peak)
        total = lax.optimization_barrier(jnp.sum(expd, axis=-1, keepdims=True))
        weights = lax.optimization_barrier((expd / total).astype(jnp.bfloat16)).astype(jnp.float32)
        mixed = jnp.einsum('rkgp,pkd->rkgd', weights, cache_values)
        log_total = peak[..., 0] + jnp.log(total[..., 0])
        return (mixed.reshape(block, HQ * HD).astype(jnp.bfloat16), log_total.reshape(block, HQ))
    mixed, log_total = lax.map(attend_block, blocks)
    mixed = mixed.reshape(ROWS, HQ * HD)
    log_total = log_total.reshape(ROWS, HQ)
    row_ids = jnp.arange(ROWS, dtype=jnp.int32)
    owner = (row_ids // LMAX).astype(jnp.int32)
    is_live = row_ids % LMAX < lengths[owner]
    prefix_out = jnp.where(is_live[:, None], mixed, jnp.zeros_like(mixed))
    prefix_lse = jnp.where(is_live[:, None], log_total, jnp.zeros_like(log_total))
    return (prefix_out, prefix_lse)
```

```python
import functools

import jax
import jax.numpy as jnp
from jax import lax
from jax.experimental import pallas as pl
from jax.experimental.pallas import tpu as pltpu
from jax.sharding import PartitionSpec as P

MESH = pl.DeviceIdType.MESH

HD = 128
COMPL = 4


rope_base = 500000.0
norm_eps = 1e-05


def rotate(field, positions):
    half = field.shape[-1] // 2
    exponents = jnp.arange(half, dtype=jnp.float32) * (2.0 / field.shape[-1])
    freqs = jnp.exp(-exponents * jnp.log(jnp.float32(rope_base)))
    angles = positions.astype(jnp.float32)[:, None] * freqs[None, :]
    cosine = jnp.cos(angles)[:, None, :]
    sine = jnp.sin(angles)[:, None, :]
    first = field[..., :half]
    second = field[..., half:]
    return jnp.concatenate(
        [first * cosine - second * sine, second * cosine + first * sine], axis=-1
    )


def length_of(owner, lengths):
    table = jnp.arange(lengths.shape[0], dtype=jnp.int32)
    return jnp.sum(jnp.where(owner[:, None] == table[None, :], lengths[None, :], 0), axis=1)


def attend_kernel(heads, group, live_ref, q_ref, k_ref, v_ref, out_ref, lse_ref):
    step = pl.program_id(0)
    coeff = HD ** (-0.5) * 1.4426950408889634
    live = live_ref[...] > 0.0
    lane = lax.broadcasted_iota(jnp.int32, lse_ref.shape, 1)
    lse = lse_ref[...]
    for h in range(heads):
        cols = slice(h * HD, (h + 1) * HD)
        scores = lax.dot_general(
            q_ref[:, cols], k_ref[...], (((1,), (1,)), ((), ())), preferred_element_type=jnp.float32
        )
        peak = jnp.max(scores, axis=1, keepdims=True)
        expd = jnp.exp2(scores * coeff - peak * coeff)
        total = jnp.sum(expd, axis=1, keepdims=True)
        mixed = jnp.dot(expd.astype(jnp.bfloat16), v_ref[...], preferred_element_type=jnp.float32)
        mixed = mixed / total
        out_ref[:, cols] = jnp.where(live, mixed, 0.0).astype(jnp.bfloat16)
        value = jnp.where(live, peak * HD ** (-0.5) + jnp.log(total), 0.0)
        lse = jnp.where(lane == step * heads + h, value, lse)
    lse_ref[...] = lse


def attend(query_rows, keys, values, row_live, kv_heads, k_base=0, v_base=0):
    rows, width = query_rows.shape
    prompt = keys.shape[0]
    q_heads = width // HD
    group = q_heads // kv_heads
    heads = 4
    live = row_live.astype(jnp.float32)[:, None]
    return pl.pallas_call(
        functools.partial(attend_kernel, heads, group),
        grid=(q_heads // heads,),
        out_shape=(
            jax.ShapeDtypeStruct((rows, width), jnp.bfloat16),
            jax.ShapeDtypeStruct((rows, q_heads), jnp.float32),
        ),
        in_specs=[
            pl.BlockSpec((rows, 1), lambda i: (0, 0)),
            pl.BlockSpec((rows, heads * HD), lambda i: (0, i)),
            pl.BlockSpec((prompt, HD), lambda i: (0, k_base + i * heads // group)),
            pl.BlockSpec((prompt, HD), lambda i: (0, v_base + i * heads // group)),
        ],
        out_specs=(
            pl.BlockSpec((rows, heads * HD), lambda i: (0, i)),
            pl.BlockSpec((rows, q_heads), lambda i: (0, 0)),
        ),
        compiler_params=pltpu.CompilerParams(vmem_limit_bytes=48 * 1024 * 1024),
    )(live, query_rows, keys, values)


def live_rows(lengths, my_index, rows_here, group_size):
    most_rows = rows_here * group_size // COMPL
    row_ids = my_index * rows_here + jnp.arange(rows_here, dtype=jnp.int32)
    return row_ids % most_rows < length_of(row_ids // most_rows, lengths)


def hello():
    groups, fsdp, mp, sub = (lax.axis_index(a) for a in ("groups", "fsdp", "mp", "sub"))
    depth = lax.axis_size("fsdp")
    barrier = pltpu.get_barrier_semaphore()
    count = 0
    for dz in range(depth):
        for dx in range(2):
            for dc in range(2):
                if (dz, dx, dc) == (0, 0, 0):
                    continue
                target = (groups, lax.rem(fsdp + dz, depth), lax.rem(mp + dx, 2), lax.rem(sub + dc, 2))
                pl.semaphore_signal(barrier, inc=1, device_id=target, device_id_type=MESH)
                count += 1
    pl.semaphore_signal(barrier, inc=1, device_id=(1 - groups, fsdp, mp, sub), device_id_type=MESH)
    pl.semaphore_wait(barrier, count + 1)


def move_kernel(
    x_ref, kw_ref, vw_ref, xin, kwo, vwo, relay,
    relay_send, relay_recv, x_send, x_recv, x_local, w_send, w_recv, f_send, f_recv,
):
    groups, fsdp, mp, sub = (lax.axis_index(a) for a in ("groups", "fsdp", "mp", "sub"))
    depth = lax.axis_size("fsdp")
    parts = 2 * depth // 2
    width = x_ref.shape[1] // parts
    hello()
    mine = sub == mp

    def relay_copy(j):
        return pltpu.make_async_remote_copy(
            src_ref=x_ref.at[:, pl.ds(j * width, width)],
            dst_ref=relay.at[j],
            send_sem=relay_send.at[j],
            recv_sem=relay_recv.at[j],
            device_id=(groups, fsdp, 1 - mp, 1 - sub),
            device_id_type=MESH,
        )

    def order(n):
        return parts - 1 - n

    half = kw_ref.shape[0] // 2
    near = pl.ds(pl.multiple_of(groups * half, half), half)

    def weight_copy(i, src, dst):
        return pltpu.make_async_remote_copy(
            src_ref=src.at[near, :], dst_ref=dst.at[near, :],
            send_sem=w_send.at[i], recv_sem=w_recv.at[i],
            device_id=(groups, fsdp, 1 - mp, sub), device_id_type=MESH,
        )

    def weight_forward(i, dst):
        return pltpu.make_async_remote_copy(
            src_ref=dst.at[near, :], dst_ref=dst.at[near, :],
            send_sem=f_send.at[i], recv_sem=f_recv.at[i],
            device_id=(1 - groups, fsdp, mp, sub), device_id_type=MESH,
        )

    def target(j):
        return (depth // 2) * sub + j // 2, j % 2

    def chunk_copy(j, src):
        tz, tc = target(j)
        return pltpu.make_async_remote_copy(
            src_ref=src, dst_ref=xin.at[fsdp], send_sem=x_send.at[j], recv_sem=x_recv.at[fsdp],
            device_id=(groups, tz, mp, tc), device_id_type=MESH,
        )

    def send_chunk(j, src):
        tz, tc = target(j)
        here = jnp.logical_and(tz == fsdp, tc == sub)

        @pl.when(here)
        def _():
            pltpu.make_async_copy(src, xin.at[fsdp], x_local).start()

        @pl.when(jnp.logical_not(here))
        def _():
            chunk_copy(j, src).start()

    def finish_chunk(j, src):
        tz, tc = target(j)
        here = jnp.logical_and(tz == fsdp, tc == sub)

        @pl.when(here)
        def _():
            pltpu.make_async_copy(src, xin.at[fsdp], x_local).wait()

        @pl.when(jnp.logical_not(here))
        def _():
            chunk_copy(j, src).wait_send()

    weights = ((kw_ref, kwo), (vw_ref, vwo))

    @pl.when(jnp.logical_not(mine))
    def _():
        for n in range(parts):
            relay_copy(order(n)).start()

    @pl.when(mine)
    def _():
        for n in range(parts):
            j = order(n)
            send_chunk(j, x_ref.at[:, pl.ds(j * width, width)])

    for i, (src, dst) in enumerate(weights):
        weight_copy(i, src, dst).start()

    @pl.when(jnp.logical_not(mine))
    def _():
        for n in range(parts):
            j = order(n)
            relay_copy(j).wait_recv()
            send_chunk(j, relay.at[j])

    for i, (src, dst) in enumerate(weights):
        weight_copy(i, src, dst).wait_recv()
        weight_forward(i, dst).start()

    @pl.when(mine)
    def _():
        for n in range(parts):
            j = order(n)
            finish_chunk(j, x_ref.at[:, pl.ds(j * width, width)])

    @pl.when(jnp.logical_not(mine))
    def _():
        for n in range(parts):
            j = order(n)
            relay_copy(j).wait_send()
            finish_chunk(j, relay.at[j])

    for z in range(depth):
        here = jnp.logical_and(fsdp == z, fsdp // (depth // 2) == sub)

        @pl.when(jnp.logical_not(here))
        def _():
            pltpu.make_async_remote_copy(
                src_ref=xin.at[z], dst_ref=xin.at[z], send_sem=x_send.at[0], recv_sem=x_recv.at[z],
                device_id=(groups, z, mp, fsdp // (depth // 2)), device_id_type=MESH,
            ).wait_recv()

    far = pl.ds(pl.multiple_of((1 - groups) * half, half), half)
    for i, (src, dst) in enumerate(weights):
        weight_copy(i, src, dst).wait_send()
        weight_forward(i, dst).wait_send()
        pltpu.make_async_remote_copy(
            src_ref=dst.at[far, :], dst_ref=dst.at[far, :],
            send_sem=f_send.at[i], recv_sem=f_recv.at[i],
            device_id=(1 - groups, fsdp, mp, sub), device_id_type=MESH,
        ).wait_recv()


def move(prompt_x, key_weight, value_weight):
    depth = lax.axis_size("fsdp")
    rows = prompt_x.shape[0]
    width = key_weight.shape[0]
    parts = prompt_x.shape[1] // width
    anywhere = pl.BlockSpec(memory_space=pl.ANY)
    dma = pltpu.SemaphoreType.DMA
    return pl.pallas_call(
        move_kernel,
        out_shape=(
            jax.ShapeDtypeStruct((depth, rows, width), jnp.bfloat16),
            jax.ShapeDtypeStruct(key_weight.shape, jnp.bfloat16),
            jax.ShapeDtypeStruct(value_weight.shape, jnp.bfloat16),
            jax.ShapeDtypeStruct((parts, rows, width), jnp.bfloat16),
        ),
        in_specs=[anywhere] * 3,
        out_specs=(anywhere,) * 4,
        scratch_shapes=[
            dma((parts,)), dma((parts,)), dma((parts,)), dma((depth,)), dma(()),
            dma((2,)), dma((2,)), dma((2,)), dma((2,)),
        ],
        compiler_params=pltpu.CompilerParams(collective_id=0, has_side_effects=True),
    )(prompt_x, key_weight, value_weight)


def body_split(queries, lengths, prompt_x, norm_gain, key_weight, value_weight):
    depth = lax.axis_size("fsdp")
    fsdp, mp, sub = (lax.axis_index(a) for a in ("fsdp", "mp", "sub"))
    my_index = fsdp * 2 + sub
    prompt_rows = prompt_x.shape[0]
    features, kv_width = key_weight.shape
    kv_heads = kv_width // HD
    widened = prompt_x.astype(jnp.float32)
    squares = jnp.sum(widened * widened, axis=1)
    squares = lax.all_gather(squares, ("mp", "fsdp", "sub"), axis=0, tiled=False)
    squares = squares.reshape(2, depth, 2, prompt_rows).sum(axis=0)
    squares = lax.dynamic_index_in_dim(squares, mp, axis=1, keepdims=False).reshape(depth * prompt_rows)
    scale = lax.rsqrt(squares / norm_gain.shape[0] + norm_eps)
    gathered, other_key, other_value, _ = move(prompt_x, key_weight, value_weight)
    gain = lax.dynamic_slice_in_dim(norm_gain, my_index * features, features)
    gathered = gathered.reshape(depth * prompt_rows, features).astype(jnp.float32)
    normed = (gathered * scale[:, None] * gain[None, :]).astype(jnp.bfloat16)
    weights = jnp.concatenate([key_weight, value_weight, other_key, other_value], axis=1)
    summed = lax.psum_scatter(
        jnp.dot(normed, weights, preferred_element_type=jnp.float32),
        ("fsdp", "sub"), scatter_dimension=0, tiled=True,
    )
    rows = summed.shape[0]
    positions = (fsdp * 2 + mp) * prompt_rows + sub * rows + jnp.arange(rows, dtype=jnp.int32)
    own_keys, own_values, far_keys, far_values = (
        summed[:, i * kv_width : (i + 1) * kv_width] for i in range(4)
    )
    turn = lambda keys: rotate(keys.reshape(rows, kv_heads, HD), positions).reshape(rows, kv_width)
    near = jnp.concatenate([turn(own_keys), own_values], axis=1).astype(jnp.bfloat16)
    far = jnp.concatenate([turn(far_keys), far_values], axis=1).astype(jnp.bfloat16)
    arrived = lax.ppermute(far, "mp", [(0, 1), (1, 0)])
    both = jnp.concatenate([near, arrived], axis=0)
    cache = lax.all_gather(both, ("fsdp", "sub"), axis=0, tiled=True)
    live = live_rows(lengths, my_index, queries.shape[0], depth * 2)
    return attend(queries, cache, cache, live, kv_heads, 0, kv_heads)


def body(queries, lengths, prompt_x, norm_gain, key_weight, value_weight):
    group_size = lax.axis_size(("fsdp", "sub"))
    my_index = lax.axis_index(("fsdp", "sub"))
    prompt_rows = prompt_x.shape[0]
    kv_width = key_weight.shape[1]
    kv_heads = kv_width // HD
    full_rows = lax.all_gather(prompt_x, "mp", axis=1, tiled=True)
    widened = full_rows.astype(jnp.float32)
    mean_square = jnp.mean(widened * widened, axis=1, keepdims=True)
    normed = (widened * lax.rsqrt(mean_square + norm_eps) * norm_gain[None, :]).astype(jnp.bfloat16)
    slices = lax.all_to_all(normed, ("fsdp", "sub"), split_axis=1, concat_axis=0, tiled=True)
    joined_weights = jnp.concatenate([key_weight, value_weight], axis=1)
    summed = lax.psum_scatter(
        jnp.dot(slices, joined_weights, preferred_element_type=jnp.float32),
        ("fsdp", "sub"),
        scatter_dimension=0,
        tiled=True,
    )
    raw_keys = summed[:, :kv_width]
    raw_values = summed[:, kv_width:]
    positions = my_index * prompt_rows + jnp.arange(prompt_rows, dtype=jnp.int32)
    cache_keys = (
        rotate(raw_keys.reshape(prompt_rows, kv_heads, HD), positions)
        .reshape(prompt_rows, kv_width)
        .astype(jnp.bfloat16)
    )
    cache_values = raw_values.astype(jnp.bfloat16)
    all_keys, all_values = (
        lax.all_gather(cache_keys, ("fsdp", "sub"), axis=0, tiled=True),
        lax.all_gather(cache_values, ("fsdp", "sub"), axis=0, tiled=True),
    )
    live = live_rows(lengths, my_index, queries.shape[0], group_size)
    return attend(queries, all_keys, all_values, live, kv_heads)


def solution(mesh):
    sizes = mesh.shape
    split = sizes["mp"] == 2 and sizes["sub"] == 2 and sizes["groups"] == 2 and sizes["fsdp"] == 4
    return jax.shard_map(
        body_split if split else body,
        mesh=mesh,
        in_specs=(
            P(("groups", "fsdp", "sub"), "mp"),
            P("groups"),
            P(("groups", "fsdp", "sub"), "mp"),
            P(),
            P(("fsdp", "sub"), "mp"),
            P(("fsdp", "sub"), "mp"),
        ),
        out_specs=(P(("groups", "fsdp", "sub"), "mp"), P(("groups", "fsdp", "sub"), "mp")),
        check_vma=False,
    )
```

```python
import functools

import jax
import jax.numpy as jnp
from jax import lax
from jax.experimental import pallas as pl
from jax.experimental.pallas import tpu as pltpu
from jax.sharding import PartitionSpec as P

MESH = pl.DeviceIdType.MESH

HD = 128
COMPL = 4


rope_base = 500000.0
norm_eps = 1e-05


def rotate(field, positions):
    half = field.shape[-1] // 2
    exponents = jnp.arange(half, dtype=jnp.float32) * (2.0 / field.shape[-1])
    freqs = jnp.exp(-exponents * jnp.log(jnp.float32(rope_base)))
    angles = positions.astype(jnp.float32)[:, None] * freqs[None, :]
    cosine = jnp.cos(angles)[:, None, :]
    sine = jnp.sin(angles)[:, None, :]
    first = field[..., :half]
    second = field[..., half:]
    return jnp.concatenate(
        [first * cosine - second * sine, second * cosine + first * sine], axis=-1
    )


def length_of(owner, lengths):
    table = jnp.arange(lengths.shape[0], dtype=jnp.int32)
    return jnp.sum(jnp.where(owner[:, None] == table[None, :], lengths[None, :], 0), axis=1)


def attend_kernel(heads, group, live_ref, q_ref, k_ref, v_ref, out_ref, lse_ref):
    step = pl.program_id(0)
    coeff = HD ** (-0.5) * 1.4426950408889634
    live = live_ref[...] > 0.0
    lane = lax.broadcasted_iota(jnp.int32, lse_ref.shape, 1)
    lse = lse_ref[...]
    for h in range(heads):
        cols = slice(h * HD, (h + 1) * HD)
        scores = lax.dot_general(
            q_ref[:, cols], k_ref[...], (((1,), (1,)), ((), ())), preferred_element_type=jnp.float32
        )
        peak = jnp.max(scores, axis=1, keepdims=True)
        expd = jnp.exp2(scores * coeff - peak * coeff)
        total = jnp.sum(expd, axis=1, keepdims=True)
        mixed = jnp.dot(expd.astype(jnp.bfloat16), v_ref[...], preferred_element_type=jnp.float32)
        mixed = mixed / total
        out_ref[:, cols] = jnp.where(live, mixed, 0.0).astype(jnp.bfloat16)
        value = jnp.where(live, peak * HD ** (-0.5) + jnp.log(total), 0.0)
        lse = jnp.where(lane == step * heads + h, value, lse)
    lse_ref[...] = lse


def attend(query_rows, keys, values, row_live, kv_heads, k_base=0, v_base=0):
    rows, width = query_rows.shape
    prompt = keys.shape[0]
    q_heads = width // HD
    group = q_heads // kv_heads
    heads = 8 if group % 8 == 0 else 4
    live = row_live.astype(jnp.float32)[:, None]
    return pl.pallas_call(
        functools.partial(attend_kernel, heads, group),
        grid=(q_heads // heads,),
        out_shape=(
            jax.ShapeDtypeStruct((rows, width), jnp.bfloat16),
            jax.ShapeDtypeStruct((rows, q_heads), jnp.float32),
        ),
        in_specs=[
            pl.BlockSpec((rows, 1), lambda i: (0, 0)),
            pl.BlockSpec((rows, heads * HD), lambda i: (0, i)),
            pl.BlockSpec((prompt, HD), lambda i: (0, k_base + i * heads // group)),
            pl.BlockSpec((prompt, HD), lambda i: (0, v_base + i * heads // group)),
        ],
        out_specs=(
            pl.BlockSpec((rows, heads * HD), lambda i: (0, i)),
            pl.BlockSpec((rows, q_heads), lambda i: (0, 0)),
        ),
        compiler_params=pltpu.CompilerParams(vmem_limit_bytes=48 * 1024 * 1024),
    )(live, query_rows, keys, values)


def live_rows(lengths, my_index, rows_here, group_size):
    most_rows = rows_here * group_size // COMPL
    row_ids = my_index * rows_here + jnp.arange(rows_here, dtype=jnp.int32)
    return row_ids % most_rows < length_of(row_ids // most_rows, lengths)


def hello():
    groups, fsdp, mp, sub = (lax.axis_index(a) for a in ("groups", "fsdp", "mp", "sub"))
    depth = lax.axis_size("fsdp")
    barrier = pltpu.get_barrier_semaphore()
    count = 0
    for dz in range(depth):
        for dx in range(2):
            for dc in range(2):
                if (dz, dx, dc) == (0, 0, 0):
                    continue
                target = (groups, lax.rem(fsdp + dz, depth), lax.rem(mp + dx, 2), lax.rem(sub + dc, 2))
                pl.semaphore_signal(barrier, inc=1, device_id=target, device_id_type=MESH)
                count += 1
    pl.semaphore_signal(barrier, inc=1, device_id=(1 - groups, fsdp, mp, sub), device_id_type=MESH)
    pl.semaphore_wait(barrier, count + 1)


def move_kernel(
    x_ref, kw_ref, vw_ref, sq_ref, xin, kwo, vwo, sqo, relay,
    relay_send, relay_recv, x_send, x_recv, x_local, w_send, w_recv, f_send, f_recv,
    sq_send, sq_recv, sq_local,
):
    groups, fsdp, mp, sub = (lax.axis_index(a) for a in ("groups", "fsdp", "mp", "sub"))
    depth = lax.axis_size("fsdp")
    parts = 2 * depth // 2
    width = x_ref.shape[1] // parts
    hello()
    mine = sub == mp

    def relay_copy(j):
        return pltpu.make_async_remote_copy(
            src_ref=x_ref.at[:, pl.ds(j * width, width)],
            dst_ref=relay.at[j],
            send_sem=relay_send.at[j],
            recv_sem=relay_recv.at[j],
            device_id=(groups, fsdp, 1 - mp, 1 - sub),
            device_id_type=MESH,
        )

    def order(n):
        return parts - 1 - n

    half = kw_ref.shape[0] // 2
    pieces = 4
    piece = half // pieces
    weights = ((kw_ref, kwo), (vw_ref, vwo))

    def piece_rows(owner, p):
        return pl.ds(pl.multiple_of(owner * half + p * piece, piece), piece)

    def weight_copy(n):
        src, dst = weights[n // pieces]
        near = piece_rows(groups, n % pieces)
        return pltpu.make_async_remote_copy(
            src_ref=src.at[near, :], dst_ref=dst.at[near, :],
            send_sem=w_send.at[n], recv_sem=w_recv.at[n],
            device_id=(groups, fsdp, 1 - mp, sub), device_id_type=MESH,
        )

    def weight_forward(n, owner):
        dst = weights[n // pieces][1]
        near = piece_rows(owner, n % pieces)
        return pltpu.make_async_remote_copy(
            src_ref=dst.at[near, :], dst_ref=dst.at[near, :],
            send_sem=f_send.at[n], recv_sem=f_recv.at[n],
            device_id=(1 - groups, fsdp, mp, sub), device_id_type=MESH,
        )

    def pass_weight(n):
        weight_copy(n).wait_recv()
        weight_forward(n, groups).start()

    def square_copy(n):
        return pltpu.make_async_remote_copy(
            src_ref=sq_ref, dst_ref=sqo.at[mp, fsdp],
            send_sem=sq_send.at[n], recv_sem=sq_recv.at[mp, fsdp],
            device_id=(groups, n // 2, sub, n % 2), device_id_type=MESH,
        )

    def square_here(n):
        return jnp.logical_and(mine, jnp.logical_and(fsdp == n // 2, sub == n % 2))

    for n in range(2 * depth):
        @pl.when(square_here(n))
        def _():
            pltpu.make_async_copy(sq_ref, sqo.at[mp, fsdp], sq_local).start()

        @pl.when(jnp.logical_not(square_here(n)))
        def _():
            square_copy(n).start()

    def target(j):
        return (depth // 2) * sub + j // 2, j % 2

    def chunk_copy(j, src):
        tz, tc = target(j)
        return pltpu.make_async_remote_copy(
            src_ref=src, dst_ref=xin.at[fsdp], send_sem=x_send.at[j], recv_sem=x_recv.at[fsdp],
            device_id=(groups, tz, mp, tc), device_id_type=MESH,
        )

    def send_chunk(j, src):
        tz, tc = target(j)
        here = jnp.logical_and(tz == fsdp, tc == sub)

        @pl.when(here)
        def _():
            pltpu.make_async_copy(src, xin.at[fsdp], x_local).start()

        @pl.when(jnp.logical_not(here))
        def _():
            chunk_copy(j, src).start()

    def finish_chunk(j, src):
        tz, tc = target(j)
        here = jnp.logical_and(tz == fsdp, tc == sub)

        @pl.when(here)
        def _():
            pltpu.make_async_copy(src, xin.at[fsdp], x_local).wait()

        @pl.when(jnp.logical_not(here))
        def _():
            chunk_copy(j, src).wait_send()

    after = ((), (0, 1), (2, 3), (4, 5, 6, 7))

    @pl.when(jnp.logical_not(mine))
    def _():
        for n in range(parts):
            relay_copy(order(n)).start()
            for i in after[n]:
                weight_copy(i).start()
        for n in range(parts):
            j = order(n)
            relay_copy(j).wait_recv()
            send_chunk(j, relay.at[j])
            for i in after[n]:
                pass_weight(i)

    @pl.when(mine)
    def _():
        for n in range(parts):
            j = order(n)
            send_chunk(j, x_ref.at[:, pl.ds(j * width, width)])
        for i in range(2 * pieces):
            weight_copy(i).start()
        for i in range(2 * pieces):
            pass_weight(i)

    @pl.when(mine)
    def _():
        for n in range(parts):
            j = order(n)
            finish_chunk(j, x_ref.at[:, pl.ds(j * width, width)])

    @pl.when(jnp.logical_not(mine))
    def _():
        for n in range(parts):
            j = order(n)
            relay_copy(j).wait_send()
            finish_chunk(j, relay.at[j])

    for z in range(depth):
        here = jnp.logical_and(fsdp == z, fsdp // (depth // 2) == sub)

        @pl.when(jnp.logical_not(here))
        def _():
            pltpu.make_async_remote_copy(
                src_ref=xin.at[z], dst_ref=xin.at[z], send_sem=x_send.at[0], recv_sem=x_recv.at[z],
                device_id=(groups, z, mp, fsdp // (depth // 2)), device_id_type=MESH,
            ).wait_recv()

    for n in range(2 * pieces):
        weight_copy(n).wait_send()
        weight_forward(n, groups).wait_send()
        weight_forward(n, 1 - groups).wait_recv()

    for n in range(2 * depth):
        @pl.when(square_here(n))
        def _():
            pltpu.make_async_copy(sq_ref, sqo.at[mp, fsdp], sq_local).wait()

        @pl.when(jnp.logical_not(square_here(n)))
        def _():
            square_copy(n).wait_send()

    for m in range(2):
        for z in range(depth):
            here = jnp.logical_and(mine, jnp.logical_and(mp == m, fsdp == z))

            @pl.when(jnp.logical_not(here))
            def _():
                pltpu.make_async_remote_copy(
                    src_ref=sqo.at[m, z], dst_ref=sqo.at[m, z],
                    send_sem=sq_send.at[0], recv_sem=sq_recv.at[m, z],
                    device_id=(groups, z, m, mp), device_id_type=MESH,
                ).wait_recv()


def move(prompt_x, key_weight, value_weight, squares):
    depth = lax.axis_size("fsdp")
    rows = prompt_x.shape[0]
    width = key_weight.shape[0]
    parts = prompt_x.shape[1] // width
    anywhere = pl.BlockSpec(memory_space=pl.ANY)
    dma = pltpu.SemaphoreType.DMA
    return pl.pallas_call(
        move_kernel,
        out_shape=(
            jax.ShapeDtypeStruct((depth, rows, width), jnp.bfloat16),
            jax.ShapeDtypeStruct(key_weight.shape, jnp.bfloat16),
            jax.ShapeDtypeStruct(value_weight.shape, jnp.bfloat16),
            jax.ShapeDtypeStruct((2, depth) + squares.shape, jnp.float32),
            jax.ShapeDtypeStruct((parts, rows, width), jnp.bfloat16),
        ),
        in_specs=[anywhere] * 4,
        out_specs=(anywhere,) * 5,
        scratch_shapes=[
            dma((parts,)), dma((parts,)), dma((parts,)), dma((depth,)), dma(()),
            dma((8,)), dma((8,)), dma((8,)), dma((8,)), dma((2 * depth,)), dma((2, depth)), dma(()),
        ],
        compiler_params=pltpu.CompilerParams(collective_id=0, has_side_effects=True),
    )(prompt_x, key_weight, value_weight, squares)


def body_split(queries, lengths, prompt_x, norm_gain, key_weight, value_weight):
    depth = lax.axis_size("fsdp")
    fsdp, mp, sub = (lax.axis_index(a) for a in ("fsdp", "mp", "sub"))
    my_index = fsdp * 2 + sub
    prompt_rows = prompt_x.shape[0]
    features, kv_width = key_weight.shape
    kv_heads = kv_width // HD
    widened = prompt_x.astype(jnp.float32)
    squares = jnp.sum(widened * widened, axis=1)
    squares = jnp.broadcast_to(squares[None, :], (8, prompt_rows))
    gathered, other_key, other_value, squares, _ = move(prompt_x, key_weight, value_weight, squares)
    squares = squares[:, :, 0, :].sum(axis=0).reshape(depth * prompt_rows)
    scale = lax.rsqrt(squares / norm_gain.shape[0] + norm_eps)
    gain = lax.dynamic_slice_in_dim(norm_gain, my_index * features, features)
    gathered = gathered.reshape(depth * prompt_rows, features).astype(jnp.float32)
    normed = (gathered * scale[:, None] * gain[None, :]).astype(jnp.bfloat16)
    weights = jnp.concatenate([key_weight, value_weight, other_key, other_value], axis=1)
    summed = lax.psum_scatter(
        jnp.dot(normed, weights, preferred_element_type=jnp.float32),
        ("fsdp", "sub"), scatter_dimension=0, tiled=True,
    )
    rows = summed.shape[0]
    positions = (fsdp * 2 + mp) * prompt_rows + sub * rows + jnp.arange(rows, dtype=jnp.int32)
    own_keys, own_values, far_keys, far_values = (
        summed[:, i * kv_width : (i + 1) * kv_width] for i in range(4)
    )
    turn = lambda keys: rotate(keys.reshape(rows, kv_heads, HD), positions).reshape(rows, kv_width)
    near = jnp.concatenate([turn(own_keys), own_values], axis=1).astype(jnp.bfloat16)
    far = jnp.concatenate([turn(far_keys), far_values], axis=1).astype(jnp.bfloat16)
    arrived = lax.ppermute(far, "mp", [(0, 1), (1, 0)])
    both = jnp.concatenate([near, arrived], axis=0)
    cache = lax.all_gather(both, ("fsdp", "sub"), axis=0, tiled=True)
    live = live_rows(lengths, my_index, queries.shape[0], depth * 2)
    return attend(queries, cache, cache, live, kv_heads, 0, kv_heads)


def body(queries, lengths, prompt_x, norm_gain, key_weight, value_weight):
    group_size = lax.axis_size(("fsdp", "sub"))
    my_index = lax.axis_index(("fsdp", "sub"))
    prompt_rows = prompt_x.shape[0]
    kv_width = key_weight.shape[1]
    kv_heads = kv_width // HD
    full_rows = lax.all_gather(prompt_x, "mp", axis=1, tiled=True)
    widened = full_rows.astype(jnp.float32)
    mean_square = jnp.mean(widened * widened, axis=1, keepdims=True)
    normed = (widened * lax.rsqrt(mean_square + norm_eps) * norm_gain[None, :]).astype(jnp.bfloat16)
    slices = lax.all_to_all(normed, ("fsdp", "sub"), split_axis=1, concat_axis=0, tiled=True)
    joined_weights = jnp.concatenate([key_weight, value_weight], axis=1)
    summed = lax.psum_scatter(
        jnp.dot(slices, joined_weights, preferred_element_type=jnp.float32),
        ("fsdp", "sub"),
        scatter_dimension=0,
        tiled=True,
    )
    raw_keys = summed[:, :kv_width]
    raw_values = summed[:, kv_width:]
    positions = my_index * prompt_rows + jnp.arange(prompt_rows, dtype=jnp.int32)
    cache_keys = (
        rotate(raw_keys.reshape(prompt_rows, kv_heads, HD), positions)
        .reshape(prompt_rows, kv_width)
        .astype(jnp.bfloat16)
    )
    cache_values = raw_values.astype(jnp.bfloat16)
    all_keys, all_values = (
        lax.all_gather(cache_keys, ("fsdp", "sub"), axis=0, tiled=True),
        lax.all_gather(cache_values, ("fsdp", "sub"), axis=0, tiled=True),
    )
    live = live_rows(lengths, my_index, queries.shape[0], group_size)
    return attend(queries, all_keys, all_values, live, kv_heads)


def solution(mesh):
    sizes = mesh.shape
    split = sizes["mp"] == 2 and sizes["sub"] == 2 and sizes["groups"] == 2 and sizes["fsdp"] == 4
    return jax.shard_map(
        body_split if split else body,
        mesh=mesh,
        in_specs=(
            P(("groups", "fsdp", "sub"), "mp"),
            P("groups"),
            P(("groups", "fsdp", "sub"), "mp"),
            P(),
            P(("fsdp", "sub"), "mp"),
            P(("fsdp", "sub"), "mp"),
        ),
        out_specs=(P(("groups", "fsdp", "sub"), "mp"), P(("groups", "fsdp", "sub"), "mp")),
        check_vma=False,
    )
```
